128 devices in a mesh: grp: 8 (over y, core), dev: 16 (over z, x).
Axes of the slice: x: 4, y: 4, z: 4, core: 2. Of those that a mesh axis runs over, the one named last changes fastest.
Arguments:
- blocks: float32 [32768, 128, 128], P(('grp', 'dev')), may hold values from -0.0625 to 0.0625
- panel: float32 [262144, 64], P(('grp', 'dev')), may hold values from -6 to 6
- block_rows: int32 [32768], P(('grp', 'dev')), may hold values from 0 to 511, as said below
- block_cols: int32 [32768], P(('grp', 'dev')), may hold values from 0 to 15
Outputs:
- basis: float32 [65536, 64], P(('grp', 'dev'))
- r_factor: float32 [64, 64], replicated
The draws below stay inside these ranges and needn't reach their ends.
Inputs may be any that keep to these rules, and one draw needn't show every extreme that they name: The blocks held by one device are distinct (block_rows, block_cols) pairs. Block row i belongs to device i // 4; among the blocks of one device at most 2 distinct block rows belong to any one device, and in every draw some device's blocks reach 2 distinct block rows of one device.
All inputs are finite; a program needn't handle non-finite values.
Results may differ from the reference program's by a relative error of at most 0.0001.
Values sent between devices are 32-bit elements; how exact they have to be, the bound alone decides.
A program may use at most 128 MiB of HBM per device.

```python
import jax
import jax.numpy as jnp
from jax import lax

BS = 128
RANK = 64
NB_DEV = 256
CB_DEV = 16
RB_DEV = 4
CAP = 2
NRB = 512
NBLK = 32768
NCB = 2048
N_GRP = 8
N_DEV = 16


def layout_helper(key):
    dest_count = N_GRP * N_DEV
    positions = dest_count * CAP * CB_DEV

    def one_device(sub):
        k_cand, k_weight, k_score, k_force = jax.random.split(sub, 4)
        cand_score = jax.random.randint(k_cand, (dest_count, RB_DEV), 0, 2 ** 20) * RB_DEV + jnp.arange(RB_DEV, dtype=jnp.int32)[None, :]
        order = jnp.argsort(cand_score, axis=1, stable=True)[:, :CAP].astype(jnp.int32)
        cand_rows = (jnp.arange(dest_count, dtype=jnp.int32)[:, None] * RB_DEV + order).reshape(-1)
        weight = jax.random.randint(k_weight, (dest_count,), 0, 2)
        place = jnp.arange(positions, dtype=jnp.int32)
        dest_of = place // (CAP * CB_DEV)
        forced = jax.random.randint(k_force, (), 0, dest_count)
        score = jax.random.randint(k_score, (positions,), 0, 2 ** 14) + weight[dest_of] * 2 ** 12
        score = score + jnp.where((dest_of == forced) & (place % CB_DEV == 0), 2 ** 17, 0)
        score = score * positions + place
        _, picked = lax.top_k(score, NB_DEV)
        picked = picked.astype(jnp.int32)
        return (cand_rows[picked // CB_DEV], picked % CB_DEV)
    keys = jax.random.split(key, dest_count)
    rows_all, cols_all = jax.vmap(one_device)(keys)
    return (rows_all.reshape(-1).astype(jnp.int32), cols_all.reshape(-1).astype(jnp.int32))


def draw_block_rows(key, part):
    return layout_helper(key)[0]


def draw_block_cols(key, part):
    return layout_helper(key)[1]


def levels(rng, dims, cuts, least, top_value):
    factor_of, own = 1.0, jax.random.fold_in(rng, 6)
    for dim, parts in cuts:
        draws = jnp.exp(jax.random.uniform(jax.random.fold_in(own, dim), (parts,), jnp.float32, least / len(cuts), top_value / len(cuts)))
        factor_of = factor_of * jnp.repeat(draws, dims[dim] // parts).reshape([-1 if axis == dim else 1 for axis in range(len(dims))])
    return factor_of


def noise(rng, extent, width, most, cuts=(), held_as=jnp.bfloat16):
    entries = jax.random.normal(rng, extent, jnp.float32) * width
    if len(cuts) > 0:
        entries = levels(rng, extent, cuts, -0.22, 0.18) * entries
    return jnp.clip(entries, min=-most, max=most).astype(held_as)


def setup_inputs(seed: int = 0) -> dict:
    key_list = jax.random.split(jax.random.key(seed), 5)
    blocks = noise(key_list[0], (NBLK, BS, BS), (NB_DEV * BS // RB_DEV) ** -0.5, 0.0625, ((0, 128),), jnp.float32)
    panel = noise(key_list[1], (NCB * BS, RANK), 1.0, 6.0, ((0, 128),), jnp.float32)
    block_rows = draw_block_rows(jax.random.fold_in(key_list[4], 71), 0)
    block_cols = draw_block_cols(jax.random.fold_in(key_list[4], 71), 0)
    return {"blocks": blocks, "panel": panel, "block_rows": block_rows, "block_cols": block_cols}


def reference(blocks, panel, block_rows, block_cols):
    dev_count = N_GRP * N_DEV
    block_size = blocks.shape[1]
    rank_cols = panel.shape[1]
    blocks_dev = blocks.reshape(dev_count, NB_DEV, block_size, block_size)
    rows_dev = block_rows.reshape(dev_count, NB_DEV)
    cols_dev = block_cols.reshape(dev_count, NB_DEV)
    panel_dev = panel.reshape(dev_count, CB_DEV, block_size, rank_cols)

    def add_device(accum, item):
        values, rows_here, cols_here, panel_here = item
        chosen = panel_here[cols_here]
        partial_sum = jnp.einsum('bij,bjr->bir', values, chosen, precision=lax.Precision.HIGHEST)
        return (accum.at[rows_here].add(partial_sum), None)
    start_acc = jnp.zeros((NRB, block_size, rank_cols), jnp.float32)
    accum, _ = lax.scan(add_device, start_acc, (blocks_dev, rows_dev, cols_dev, panel_dev))
    product = accum.reshape(NRB * block_size, rank_cols)
    gram = jnp.dot(product.T, product, precision=lax.Precision.HIGHEST) / (NRB * block_size)
    lower = jnp.linalg.cholesky(gram)
    basis = lax.linalg.triangular_solve(lower, product.T, left_side=True, lower=True).T
    return (basis, lower.T)
```

```python
import functools

import jax
import jax.numpy as jnp
from jax import lax
from jax.experimental import pallas as pl
from jax.experimental.pallas import tpu as pltpu
from jax.sharding import PartitionSpec as P

MESH = pl.DeviceIdType.MESH
F32 = jnp.float32
BF16 = jnp.bfloat16
NB = 256
BS = 128
RANK = 64
ROWS = 4
NRB = 512
HALF = BS // 2
PK = HALF // 2
CHUNKS = 8
PER = NB // CHUNKS
GROUP = 8
AXES = ("x", "y", "z")
STRIDE = {"x": 1, "z": 4, "y": 32}
FLOWS = (
    (0, 0, 6, "xyz"),
    (0, 6, 11, "yzx"),
    (0, 11, 16, "zxy"),
    (1, 0, 5, "xyz"),
    (1, 5, 11, "yzx"),
    (1, 11, 16, "zxy"),
)
NF = len(FLOWS)
ORDER = (2, 3, 1, 0)


def coords():
    g, d = lax.axis_index("grp"), lax.axis_index("dev")
    return {"x": d % 4, "z": d // 4, "y": g // 2, "c": g % 2}


def device(me, **moved):
    at = dict(me)
    at.update(moved)
    return (at["y"] * 2 + at["c"], at["z"] * 4 + at["x"])


def neighbour(me, axis, step):
    return device(me, **{axis: (me[axis] + step + 4) % 4})


def groups_of(first, end):
    out, tile = [], first
    while tile < end:
        row, within = divmod(tile, 4)
        count = min(4 - within, end - tile)
        out.append((row, within, count, tile - first))
        tile += count
    return out


def remote(src, dst, send, recv, to):
    return pltpu.make_async_remote_copy(
        src_ref=src, dst_ref=dst, send_sem=send, recv_sem=recv, device_id=to, device_id_type=MESH
    )


def reduce_kernel(*refs):
    meta, panel, blocks, prod_ref, gram_ref = refs[:5]
    refs = list(refs[5:])
    held, weights, sums = refs[:3]
    refs = refs[3:]
    mine_out, pair_in, a1, b1, b2, s1, a2, b12, b22, q2, c3 = (
        refs[NF * i : NF * (i + 1)] for i in range(11)
    )
    (gbuf, hbm_sem, pair_s, pair_r, one_s, one_r, two_s, two_r, three_s, three_r, gram_s, gram_r) = refs[NF * 11 :]
    me = coords()

    loads = []
    for half in range(2):
        for c in range(CHUNKS):
            part = (pl.ds(c * PER, PER), pl.ds(half * HALF, HALF))
            copy = pltpu.make_async_copy(blocks.at[part], held.at[part], hbm_sem.at[half, c])
            copy.start()
            loads.append(copy)

    barrier = pltpu.get_barrier_semaphore()
    peers = [device(me, c=1 - me["c"])]
    for axis in AXES:
        peers += [neighbour(me, axis, step) for step in (1, 2, 3)]
    for peer in peers:
        pl.semaphore_signal(barrier, inc=1, device_id=peer, device_id_type=MESH)

    lane_low = lax.broadcasted_iota(jnp.int32, (PK, BS), 1) < RANK

    def prepare(c, _):
        p = panel[pl.ds(pl.multiple_of(c * BS, BS), BS), :]
        high = p.astype(BF16)
        low = (p - high.astype(F32)).astype(BF16)
        both = jnp.concatenate([high, low], axis=1)
        weights[c, :BS, :] = both
        weights[c, BS:, :] = both
        return 0

    lax.fori_loop(0, 16, prepare, 0)
    for half in range(2):
        sums[half, NB] = jnp.zeros((PK, BS), F32)

    def multiply(half, c):
        loads[half * CHUNKS + c].wait()

        def step(g, _):
            base = c * PER + g * GROUP
            out = []
            for i in range(GROUP):
                k = base + i
                x = held[k, half * HALF : (half + 1) * HALF, :]
                high = x.astype(BF16)
                low = (x - high.astype(F32)).astype(BF16)
                left = jnp.concatenate([high, low], axis=1)
                u = jnp.dot(left, weights[meta[k]], preferred_element_type=F32)
                top, bottom = u[:PK], u[PK:]
                out.append(
                    jnp.where(lane_low, top, bottom)
                    + pltpu.roll(jnp.where(lane_low, bottom, top), RANK, 1)
                )
            for i in range(GROUP):
                k = base + i
                sums[half, k] = out[i] + sums[half, meta[NB + k]]
            return 0

        lax.fori_loop(0, PER // GROUP, step, 0)

    def owner(f, core, ua, ub, uc):
        half, _, _, order = FLOWS[f]
        sign = 1 if half == 0 else -1
        at = core * 16
        for axis, u in zip(order, (ua, ub, uc)):
            at = at + STRIDE[axis] * ((me[axis] + (sign * u) % 4) % 4)
        return at

    def own_rows(f, core, ua, ub, uc):
        half, first, end, _ = FLOWS[f]
        o = owner(f, core, ua, ub, uc)
        for row, within, count, offset in groups_of(first, end):
            at = meta[2 * NB + o * ROWS + row]
            yield offset, count, sums[half, at, within * 8 : (within + count) * 8, :]

    def neigh(f, order_at, direction):
        half, _, _, order = FLOWS[f]
        sign = 1 if half == 0 else -1
        return neighbour(me, order[order_at], sign * direction)

    started = []

    def go(copy):
        copy.start()
        started.append(copy)
        return copy

    def pair_copy(f, ua):
        return remote(
            mine_out[f].at[ua], pair_in[f].at[ua], pair_s.at[f, ua], pair_r.at[f, ua], device(me, c=1 - me["c"])
        )

    def fill(f, ua):
        for ub in range(4):
            for uc in range(4):
                for offset, count, value in own_rows(f, 1 - me["c"], ua, ub, uc):
                    mine_out[f][ua, ub, uc, offset * 8 : (offset + count) * 8, :] = value
        return go(pair_copy(f, ua))

    def one_copy(f, kind, ub):
        ua, buf, direction = ((2, a1, 1), (3, b1, -1), (1, b2, 1))[kind]
        return remote(
            pair_in[f].at[ua, ub], buf[f].at[ub], one_s.at[f, kind, ub], one_r.at[f, kind, ub], neigh(f, 0, direction)
        )

    def chip_sum(f, ua, ub, extra, out):
        for uc in range(4):
            for offset, count, value in own_rows(f, me["c"], ua, ub, uc):
                rows = slice(offset * 8, (offset + count) * 8)
                value = value + pair_in[f][ua, ub, uc, rows, :]
                for e in extra:
                    value = value + e[f][ub, uc, rows, :]
                out[uc, rows, :] = value

    def begin(flows):
        pairs = {}
        for ua in ORDER:
            for f in flows:
                pairs[f, ua] = fill(f, ua)
        for kind, ua in ((0, 2), (1, 3)):
            for f in flows:
                pairs[f, ua].wait_recv()
                for ub in ORDER:
                    chip_sum(f, ua, ub, (), pair_in[f].at[ua, ub])
                    go(one_copy(f, kind, ub))
        return pairs

    for c in range(CHUNKS):
        multiply(0, c)
    pl.semaphore_wait(barrier, len(peers))
    pairs = begin((0, 1, 2))
    for c in range(CHUNKS):
        multiply(1, c)
    pairs.update(begin((3, 4, 5)))

    for ub in ORDER:
        for f in range(NF):
            if ub == ORDER[0]:
                pairs[f, 1].wait_recv()
            one_copy(f, 0, ub).wait_recv()
            chip_sum(f, 1, ub, (a1,), pair_in[f].at[1, ub])
            go(one_copy(f, 2, ub))

    def two_copy(f, kind):
        ub, buf, direction = ((2, a2, 1), (3, b12, -1), (1, b22, 1))[kind]
        return remote(s1[f].at[ub], buf[f], two_s.at[f, kind], two_r.at[f, kind], neigh(f, 1, direction))

    def three_copy(f, uc):
        return remote(q2[f].at[uc], c3[f].at[uc - 1], three_s.at[f, uc - 1], three_r.at[f, uc - 1], neigh(f, 2, uc))

    for ub in ORDER:
        for f in range(NF):
            if ub == ORDER[0]:
                pairs[f, 0].wait_recv()
            one_copy(f, 1, ub).wait_recv()
            one_copy(f, 2, ub).wait_recv()
            chip_sum(f, 0, ub, (b1, b2), s1[f].at[ub])
            if ub == 2:
                go(two_copy(f, 0))
            elif ub == 3:
                go(two_copy(f, 1))
            elif ub == 1:
                two_copy(f, 0).wait_recv()
                s1[f][1] = s1[f][1] + a2[f][...]
                go(two_copy(f, 2))
    for f in range(NF):
        two_copy(f, 1).wait_recv()
        two_copy(f, 2).wait_recv()
        q2[f][...] = s1[f][0] + b12[f][...] + b22[f][...]
        for uc in (2, 1, 3):
            go(three_copy(f, uc))
    for f in range(NF):
        half, first, end, _ = FLOWS[f]
        for uc in (1, 2, 3):
            three_copy(f, uc).wait_recv()
        prod_ref[half * 128 + first * 8 : half * 128 + end * 8, :] = (
            q2[f][0] + c3[f][0] + (c3[f][1] + c3[f][2])
        )

    prod = prod_ref[...]
    both = lax.dot_general(
        prod, prod, (((0,), (0,)), ((), ())), precision=lax.Precision.HIGHEST, preferred_element_type=F32
    )
    upper, lower = both[:RANK], both[RANK:]
    in_low = upper + pltpu.roll(lower, RANK, 1)
    in_high = pltpu.roll(upper, RANK, 1) + lower
    gbuf[0, 0] = jnp.where(lane_low, in_low[:PK], in_high[PK:]) * (1.0 / (NRB * BS))

    copy = go(remote(gbuf.at[0, 0], gbuf.at[0, 1], gram_s.at[0, 0], gram_r.at[0, 0], device(me, c=1 - me["c"])))
    copy.wait_recv()
    total = gbuf[0, 0] + gbuf[0, 1]
    for i, axis in enumerate(AXES):
        gbuf[i + 1, 0] = total
        copies = [
            go(
                remote(
                    gbuf.at[i + 1, 0],
                    gbuf.at[i + 1, step],
                    gram_s.at[i + 1, step - 1],
                    gram_r.at[i + 1, step - 1],
                    neighbour(me, axis, step),
                )
            )
            for step in (1, 2, 3)
        ]
        for copy in copies:
            copy.wait_recv()
        total = (gbuf[i + 1, 0] + gbuf[i + 1, 2]) + (gbuf[i + 1, 1] + gbuf[i + 1, 3])
    gram_ref[...] = total
    for copy in started:
        copy.wait_send()


def factor_kernel(gram_ref, prod_ref, basis_ref, r_ref):
    lane = lax.broadcasted_iota(jnp.int32, (8, BS), 1)
    sub = lax.broadcasted_iota(jnp.int32, (8, BS), 0)
    packed = gram_ref[...]
    turned = pltpu.roll(packed, RANK, 1)
    tiles = []
    for t in range(8):
        half = packed if t < 4 else turned
        g = half[(t % 4) * 8 : (t % 4 + 1) * 8, :]
        eye = (lane - RANK == sub + t * 8).astype(F32)
        tiles.append(jnp.where(lane < RANK, g, eye))
    diag = [jnp.ones((8, BS), F32)] * 8
    for j in range(RANK):
        tj, jj = divmod(j, 8)
        cols = {t: jnp.broadcast_to(tiles[t][:, j : j + 1], (8, BS)) for t in range(tj, 8)}
        pivot = jnp.broadcast_to(cols[tj][jj : jj + 1, :], (8, BS))
        row = jnp.broadcast_to(tiles[tj][jj : jj + 1, :], (8, BS)) / pivot
        diag[tj] = jnp.where(sub == jj, pivot, diag[tj])
        for t in range(tj, 8):
            col = jnp.where(sub > jj, cols[t], 0.0) if t == tj else cols[t]
            tiles[t] = tiles[t] - col * row
    scaled = jnp.concatenate([tiles[t] / jnp.sqrt(diag[t]) for t in range(8)], axis=0)
    lane = lax.broadcasted_iota(jnp.int32, (RANK, BS), 1)
    sub = lax.broadcasted_iota(jnp.int32, (RANK, BS), 0)
    r_ref[...] = jnp.where(lane >= sub, scaled, 0.0)[:, :RANK]
    inv_high = jnp.where(lane >= RANK, scaled, 0.0)
    inv_low = pltpu.roll(inv_high, RANK, 1)
    prod = prod_ref[...]
    for side, inv in ((0, inv_low), (1, inv_high)):
        out = lax.dot_general(
            prod, inv, (((1,), (1,)), ((), ())), precision=lax.Precision.HIGHEST, preferred_element_type=F32
        )
        for half in range(2):
            for r in range(ROWS):
                to = r * BS + half * HALF + side * PK
                basis_ref[to : to + PK, :] = out[half * BS + r * PK : half * BS + (r + 1) * PK, :]


def reduced(meta, panel, blocks):
    rows = [(end - first) * 8 for _, first, end, _ in FLOWS]

    def per_flow(*lead):
        return [pltpu.VMEM((*lead, n, BS), F32) for n in rows]

    dma = pltpu.SemaphoreType.DMA
    scratch = [
        pltpu.VMEM((NB, BS, BS), F32),
        pltpu.VMEM((16, 2 * BS, BS), BF16),
        pltpu.VMEM((2, NB + 1, PK, BS), F32),
        *per_flow(4, 4, 4),
        *per_flow(4, 4, 4),
        *per_flow(4, 4),
        *per_flow(4, 4),
        *per_flow(4, 4),
        *per_flow(4, 4),
        *per_flow(4),
        *per_flow(4),
        *per_flow(4),
        *per_flow(4),
        *per_flow(3),
        pltpu.VMEM((4, 4, PK, BS), F32),
        dma((2, CHUNKS)),
        dma((NF, 4)),
        dma((NF, 4)),
        dma((NF, 3, 4)),
        dma((NF, 3, 4)),
        dma((NF, 3)),
        dma((NF, 3)),
        dma((NF, 3)),
        dma((NF, 3)),
        dma((4, 3)),
        dma((4, 3)),
    ]
    return pl.pallas_call(
        reduce_kernel,
        out_shape=(jax.ShapeDtypeStruct((256, BS), F32), jax.ShapeDtypeStruct((PK, BS), F32)),
        in_specs=[
            pl.BlockSpec(memory_space=pltpu.SMEM),
            pl.BlockSpec(memory_space=pltpu.VMEM),
            pl.BlockSpec(memory_space=pl.ANY),
        ],
        out_specs=(pl.BlockSpec(memory_space=pltpu.VMEM), pl.BlockSpec(memory_space=pltpu.VMEM)),
        scratch_shapes=scratch,
        compiler_params=pltpu.CompilerParams(collective_id=0, has_side_effects=True, vmem_limit_bytes=60 << 20),
        name="reduce",
    )(meta, panel, blocks)


def factored(gram, prod):
    vmem = pl.BlockSpec(memory_space=pltpu.VMEM)
    return pl.pallas_call(
        factor_kernel,
        out_shape=(jax.ShapeDtypeStruct((512, RANK), F32), jax.ShapeDtypeStruct((RANK, RANK), F32)),
        in_specs=[vmem, vmem],
        out_specs=(vmem, vmem),
        compiler_params=pltpu.CompilerParams(vmem_limit_bytes=16 << 20),
        name="factor",
    )(gram, prod)


def per_device(blocks, panel, block_rows, block_cols):
    k = jnp.arange(NB, dtype=jnp.int32)
    same = (block_rows[:, None] == block_rows[None, :]) & (k[None, :] < k[:, None])
    previous = jnp.max(jnp.where(same, k[None, :], -1), axis=1)
    previous = jnp.where(previous < 0, NB, previous)
    here = block_rows[None, :] == jnp.arange(NRB, dtype=jnp.int32)[:, None]
    last = jnp.max(jnp.where(here, k[None, :], -1), axis=1)
    last = jnp.where(last < 0, NB, last)
    meta = jnp.concatenate([block_cols, previous, last])
    prod, gram = reduced(meta, panel, blocks)
    return factored(gram, prod)


def solution(mesh):
    placed = (
        P(("grp", "dev"), None, None),
        P(("grp", "dev"), None),
        P(("grp", "dev")),
        P(("grp", "dev")),
    )
    return jax.shard_map(
        per_device,
        mesh=mesh,
        in_specs=placed,
        out_specs=(P(("grp", "dev"), None), P()),
        check_vma=False,
    )
```

```python
import functools

import jax
import jax.numpy as jnp
from jax import lax
from jax.experimental import pallas as pl
from jax.experimental.pallas import tpu as pltpu
from jax.sharding import PartitionSpec as P

MESH = pl.DeviceIdType.MESH
F32 = jnp.float32
BF16 = jnp.bfloat16
NB = 256
BS = 128
RANK = 64
ROWS = 4
NRB = 512
HALF = BS // 2
PK = HALF // 2
CHUNKS = 4
PER = NB // CHUNKS
NCOL = 16
AXES = ("x", "y", "z")
STRIDE = {"x": 1, "z": 4, "y": 32}
FLOWS = (
    (0, 0, 6, "xyz"),
    (0, 6, 11, "yzx"),
    (0, 11, 16, "zxy"),
    (1, 0, 5, "xyz"),
    (1, 5, 11, "yzx"),
    (1, 11, 16, "zxy"),
)
NF = len(FLOWS)
ORDER = (2, 3, 1, 0)
SPLITS = (((0, 2), (2, 4)), ((0, 4),), ((0, 1), (1, 2), (2, 3), (3, 4)))


def coords():
    g, d = lax.axis_index("grp"), lax.axis_index("dev")
    return {"x": d % 4, "z": d // 4, "y": g // 2, "c": g % 2}


def device(me, **moved):
    at = dict(me)
    at.update(moved)
    return (at["y"] * 2 + at["c"], at["z"] * 4 + at["x"])


def neighbour(me, axis, step):
    return device(me, **{axis: (me[axis] + step + 4) % 4})


def groups_of(first, end):
    out, tile = [], first
    while tile < end:
        row, within = divmod(tile, 4)
        count = min(4 - within, end - tile)
        out.append((row, within, count, tile - first))
        tile += count
    return out


def remote(src, dst, send, recv, to):
    return pltpu.make_async_remote_copy(
        src_ref=src, dst_ref=dst, send_sem=send, recv_sem=recv, device_id=to, device_id_type=MESH
    )


def reduce_kernel(*refs):
    cols, rows_in, panel_t, blocks, out_ref = refs[:5]
    refs = list(refs[5:])
    held, weights, sums, panel, table, meta = refs[:6]
    refs = refs[6:]
    mine_out, pair_in, a1, b1, b2, s1, a2, b12, b22, q2, c3 = (
        refs[NF * i : NF * (i + 1)] for i in range(11)
    )
    (gbuf, aux_sem, hbm_sem, pair_s, pair_r, one_s, one_r, two_s, two_r, three_s, three_r, gram_s, gram_r) = refs[NF * 11 :]
    me = coords()

    panel_copy = pltpu.make_async_copy(panel_t, panel, aux_sem.at[0])
    panel_copy.start()

    def load(half, c):
        part = (pl.ds(c * PER, PER), pl.ds(half * HALF, HALF))
        return pltpu.make_async_copy(blocks.at[part], held.at[part], hbm_sem.at[half, c])

    for c in range(2):
        load(0, c).start()

    barrier = pltpu.get_barrier_semaphore()
    peers = [device(me, c=1 - me["c"])]
    for axis in AXES:
        peers += [neighbour(me, axis, step) for step in (1, 2, 3)]
    for peer in peers:
        pl.semaphore_signal(barrier, inc=1, device_id=peer, device_id_type=MESH)

    lane = lax.broadcasted_iota(jnp.int32, (BS, BS), 1)
    sub = lax.broadcasted_iota(jnp.int32, (BS, BS), 0)
    across = [jnp.broadcast_to(rows_in[:, i * BS : (i + 1) * BS].astype(F32), (BS, BS)) for i in range(2)]
    down = [x.T for x in across]
    for i in range(2):
        best = jnp.full((1, BS), -1, jnp.int32)
        for q in range(i + 1):
            same = across[i] == down[q]
            if q == i:
                same = same & (sub < lane)
            best = jnp.maximum(best, jnp.max(jnp.where(same, sub + q * BS, -1), axis=0, keepdims=True))
        table[:, i * BS : (i + 1) * BS] = jnp.where(best < 0, NB, best)
    for i in range(NRB // BS):
        best = jnp.full((1, BS), -1, jnp.int32)
        target = (lane + i * BS).astype(F32)
        for q in range(2):
            best = jnp.maximum(best, jnp.max(jnp.where(target == down[q], sub + q * BS, -1), axis=0, keepdims=True))
        table[:, NB + i * BS : NB + (i + 1) * BS] = jnp.where(best < 0, NB, best)
    table_copy = pltpu.make_async_copy(table, meta, aux_sem.at[1])
    table_copy.start()

    lane_low = lax.broadcasted_iota(jnp.int32, (PK, BS), 1) < RANK
    panel_copy.wait()

    for c in range(NCOL):
        p = panel[:, c * BS : (c + 1) * BS]
        high = p.astype(BF16).astype(F32)
        both = jnp.concatenate([high, p - high], axis=0).T.astype(BF16)
        weights[c, :BS, :] = both
        weights[c, BS:, :] = both
    for half in range(2):
        sums[half, NB] = jnp.zeros((PK, BS), F32)
    table_copy.wait()

    def multiply(half):
        def step(c, _):
            load(half, c).wait()
            if half == 0:
                ahead = c + 2
                load(ahead // CHUNKS, ahead % CHUNKS).start()
            out = []
            for i in range(PER):
                k = c * PER + i
                x = held[k, half * HALF : (half + 1) * HALF, :]
                high = x.astype(BF16)
                low = (x - high.astype(F32)).astype(BF16)
                left = jnp.concatenate([high, low], axis=1)
                u = jnp.dot(left, weights[cols[k]], preferred_element_type=F32)
                top, bottom = u[:PK], u[PK:]
                out.append(
                    jnp.where(lane_low, top, bottom)
                    + pltpu.roll(jnp.where(lane_low, bottom, top), RANK, 1)
                )
            for i in range(PER):
                k = c * PER + i
                sums[half, k] = out[i] + sums[half, meta[0, k]]
            return 0

        lax.fori_loop(0, CHUNKS, step, 0)

    def owner(f, core, ua, ub, uc):
        half, _, _, order = FLOWS[f]
        sign = 1 if half == 0 else -1
        at = core * 16
        for axis, u in zip(order, (ua, ub, uc)):
            at = at + STRIDE[axis] * ((me[axis] + (sign * u) % 4) % 4)
        return at

    def own_rows(f, core, ua, ub, uc):
        half, first, end, _ = FLOWS[f]
        o = owner(f, core, ua, ub, uc)
        for row, within, count, offset in groups_of(first, end):
            at = meta[0, NB + o * ROWS + row]
            yield offset, count, sums[half, at, within * 8 : (within + count) * 8, :]

    def neigh(f, order_at, direction):
        half, _, _, order = FLOWS[f]
        sign = 1 if half == 0 else -1
        return neighbour(me, order[order_at], sign * direction)

    started = []

    def go(copy):
        copy.start()
        started.append(copy)
        return copy

    def pair_copy(f, ua):
        return remote(
            mine_out[f].at[ua], pair_in[f].at[ua], pair_s.at[f, ua], pair_r.at[f, ua], device(me, c=1 - me["c"])
        )

    def fill(f, ua):
        for pb in range(4):
            for pc in range(4):
                for offset, count, value in own_rows(f, 1 - me["c"], ua, ORDER[pb], ORDER[pc]):
                    mine_out[f][ua, pb, pc, offset * 8 : (offset + count) * 8, :] = value
        return go(pair_copy(f, ua))

    def one_copy(f, kind, part):
        ua, buf, direction = ((2, a1, 1), (3, b1, -1), (1, b2, 1))[kind]
        lo, hi = SPLITS[kind][part]
        at = pl.ds(lo, hi - lo)
        return remote(
            pair_in[f].at[ua, at], buf[f].at[at], one_s.at[f, kind, part], one_r.at[f, kind, part], neigh(f, 0, direction)
        )

    def chip_sum(f, ua, pb, extra, out):
        for pc in range(4):
            for offset, count, value in own_rows(f, me["c"], ua, ORDER[pb], ORDER[pc]):
                rows = slice(offset * 8, (offset + count) * 8)
                value = value + pair_in[f][ua, pb, pc, rows, :]
                for e in extra:
                    value = value + e[f][pb, pc, rows, :]
                out[pc, rows, :] = value

    def begin(flows):
        pairs = {}
        for ua in ORDER:
            for f in flows:
                pairs[f, ua] = fill(f, ua)
        for kind, ua in ((0, 2), (1, 3)):
            for f in flows:
                pairs[f, ua].wait_recv()
                for part, (lo, hi) in enumerate(SPLITS[kind]):
                    for pb in range(lo, hi):
                        chip_sum(f, ua, pb, (), pair_in[f].at[ua, pb])
                    go(one_copy(f, kind, part))
        return pairs

    multiply(0)
    for c in range(2, CHUNKS):
        load(1, c).start()
    pl.semaphore_wait(barrier, len(peers))
    pairs = begin((0, 1, 2))
    multiply(1)
    pairs.update(begin((3, 4, 5)))

    for part in range(4):
        for f in range(NF):
            if part == 0:
                pairs[f, 1].wait_recv()
            if part % 2 == 0:
                one_copy(f, 0, part // 2).wait_recv()
            chip_sum(f, 1, part, (a1,), pair_in[f].at[1, part])
            go(one_copy(f, 2, part))

    def two_copy(f, kind):
        pb, buf, direction = ((0, a2, 1), (1, b12, -1), (2, b22, 1))[kind]
        return remote(s1[f].at[pb], buf[f], two_s.at[f, kind], two_r.at[f, kind], neigh(f, 1, direction))

    def three_copy(f, pc):
        return remote(q2[f].at[pc], c3[f].at[pc], three_s.at[f, pc], three_r.at[f, pc], neigh(f, 2, ORDER[pc]))

    for part in range(4):
        for f in range(NF):
            if part == 0:
                pairs[f, 0].wait_recv()
                one_copy(f, 1, 0).wait_recv()
            one_copy(f, 2, part).wait_recv()
            chip_sum(f, 0, part, (b1, b2), s1[f].at[part])
            if part < 2:
                go(two_copy(f, part))
            elif part == 2:
                two_copy(f, 0).wait_recv()
                s1[f][2] = s1[f][2] + a2[f][...]
                go(two_copy(f, 2))
    for f in range(NF):
        two_copy(f, 1).wait_recv()
        two_copy(f, 2).wait_recv()
        q2[f][...] = s1[f][3] + b12[f][...] + b22[f][...]
        for pc in range(3):
            go(three_copy(f, pc))
    for f in range(NF):
        half, first, end, _ = FLOWS[f]
        for pc in range(3):
            three_copy(f, pc).wait_recv()
        out_ref[half * 128 + first * 8 : half * 128 + end * 8, :] = (
            q2[f][3] + c3[f][0] + (c3[f][1] + c3[f][2])
        )

    prod = out_ref[:256, :]
    both = lax.dot_general(
        prod, prod, (((0,), (0,)), ((), ())), precision=lax.Precision.HIGHEST, preferred_element_type=F32
    )
    upper, lower = both[:RANK], both[RANK:]
    in_low = upper + pltpu.roll(lower, RANK, 1)
    in_high = pltpu.roll(upper, RANK, 1) + lower
    gbuf[0, 0] = jnp.where(lane_low, in_low[:PK], in_high[PK:]) * (1.0 / (NRB * BS))

    copy = go(remote(gbuf.at[0, 0], gbuf.at[0, 1], gram_s.at[0, 0], gram_r.at[0, 0], device(me, c=1 - me["c"])))
    copy.wait_recv()
    total = gbuf[0, 0] + gbuf[0, 1]
    for i, axis in enumerate(AXES):
        gbuf[i + 1, 0] = total
        copies = [
            go(
                remote(
                    gbuf.at[i + 1, 0],
                    gbuf.at[i + 1, step],
                    gram_s.at[i + 1, step - 1],
                    gram_r.at[i + 1, step - 1],
                    neighbour(me, axis, step),
                )
            )
            for step in (1, 2, 3)
        ]
        for copy in copies:
            copy.wait_recv()
        total = (gbuf[i + 1, 0] + gbuf[i + 1, 2]) + (gbuf[i + 1, 1] + gbuf[i + 1, 3])
    out_ref[256:, :] = total
    for copy in started:
        copy.wait_send()


def factor_kernel(in_ref, basis_ref, r_ref):
    lane = lax.broadcasted_iota(jnp.int32, (8, BS), 1)
    sub = lax.broadcasted_iota(jnp.int32, (8, BS), 0)
    packed = in_ref[256:, :]
    turned = pltpu.roll(packed, RANK, 1)
    tiles = []
    for t in range(8):
        half = packed if t < 4 else turned
        g = half[(t % 4) * 8 : (t % 4 + 1) * 8, :]
        eye = (lane - RANK == sub + t * 8).astype(F32)
        tiles.append(jnp.where(lane < RANK, g, eye))

    def row_of(x, j):
        return jnp.broadcast_to(x[j : j + 1, :], (8, BS))

    def column_of(x, j):
        return jnp.broadcast_to(x[:, j : j + 1], (8, BS))

    done = []
    for t in range(8):
        cols = [column_of(tiles[t], 8 * t + j) for j in range(8)]
        rest = {u: [column_of(tiles[u], 8 * t + j) for j in range(8)] for u in range(t + 1, 8)}
        forward = full = tiles[t]
        pivots = inverses = jnp.ones((8, BS), F32)
        for j in range(8):
            pivot = row_of(cols[j], j)
            inverse = 1.0 / pivot
            pivots = jnp.where(sub == j, pivot, pivots)
            inverses = jnp.where(sub == j, inverse, inverses)
            c = cols[j] * inverse
            others = jnp.where(sub == j, 0.0, c)
            for k in range(j + 1, 8):
                cols[k] = cols[k] - others * row_of(cols[k], j)
            row = row_of(full, j)
            forward = forward - jnp.where(sub > j, c, 0.0) * row
            full = full - others * row
        full = full * inverses
        rows = [row_of(full, j) for j in range(8)]
        for u in range(t + 1, 8):
            p = [rest[u][j] * rows[j] for j in range(8)]
            p = [p[0] + p[1], p[2] + p[3], p[4] + p[5], p[6] + p[7]]
            tiles[u] = tiles[u] - ((p[0] + p[1]) + (p[2] + p[3]))
        scale = lax.rsqrt(pivots)
        done.append(forward * (scale * (1.5 - 0.5 * pivots * scale * scale)))
    scaled = jnp.concatenate(done, axis=0)
    lane = lax.broadcasted_iota(jnp.int32, (RANK, BS), 1)
    sub = lax.broadcasted_iota(jnp.int32, (RANK, BS), 0)
    r_ref[...] = jnp.where(lane >= sub, scaled, 0.0)[:, :RANK]
    inverse = pltpu.roll(jnp.where(lane >= RANK, scaled, 0.0), RANK, 1)
    prod = in_ref[:256, :]
    turned = pltpu.roll(prod, RANK, 1)
    for r in range(ROWS):
        part = jnp.concatenate(
            [x[half * BS + r * PK : half * BS + (r + 1) * PK] for half in range(2) for x in (prod, turned)], axis=0
        )
        basis_ref[:, r * BS : (r + 1) * BS] = lax.dot_general(
            inverse, part, (((1,), (1,)), ((), ())), precision=lax.Precision.HIGHEST, preferred_element_type=F32
        )


def reduced(cols, rows_in, panel_t, blocks):
    rows = [(end - first) * 8 for _, first, end, _ in FLOWS]

    def per_flow(*lead):
        return [pltpu.VMEM((*lead, n, BS), F32) for n in rows]

    dma = pltpu.SemaphoreType.DMA
    scratch = [
        pltpu.VMEM((NB, BS, BS), F32),
        pltpu.VMEM((16, 2 * BS, BS), BF16),
        pltpu.VMEM((2, NB + 1, PK, BS), F32),
        pltpu.VMEM((RANK, NCOL * BS), F32),
        pltpu.VMEM((1, NB + NRB), jnp.int32),
        pltpu.SMEM((1, NB + NRB), jnp.int32),
        *per_flow(4, 4, 4),
        *per_flow(4, 4, 4),
        *per_flow(4, 4),
        *per_flow(4, 4),
        *per_flow(4, 4),
        *per_flow(4, 4),
        *per_flow(4),
        *per_flow(4),
        *per_flow(4),
        *per_flow(4),
        *per_flow(3),
        pltpu.VMEM((4, 4, PK, BS), F32),
        dma((2,)),
        dma((2, CHUNKS)),
        dma((NF, 4)),
        dma((NF, 4)),
        dma((NF, 3, 4)),
        dma((NF, 3, 4)),
        dma((NF, 3)),
        dma((NF, 3)),
        dma((NF, 3)),
        dma((NF, 3)),
        dma((4, 3)),
        dma((4, 3)),
    ]
    return pl.pallas_call(
        reduce_kernel,
        out_shape=jax.ShapeDtypeStruct((256 + PK, BS), F32),
        in_specs=[
            pl.BlockSpec(memory_space=pltpu.SMEM),
            pl.BlockSpec(memory_space=pltpu.VMEM),
            pl.BlockSpec(memory_space=pl.ANY),
            pl.BlockSpec(memory_space=pl.ANY),
        ],
        out_specs=pl.BlockSpec(memory_space=pltpu.VMEM),
        scratch_shapes=scratch,
        compiler_params=pltpu.CompilerParams(collective_id=0, has_side_effects=True, vmem_limit_bytes=60 << 20),
        name="reduce",
    )(cols, rows_in, panel_t, blocks)


def factored(result):
    vmem = pl.BlockSpec(memory_space=pltpu.VMEM)
    return pl.pallas_call(
        factor_kernel,
        out_shape=(jax.ShapeDtypeStruct((RANK, 512), F32), jax.ShapeDtypeStruct((RANK, RANK), F32)),
        in_specs=[vmem],
        out_specs=(vmem, vmem),
        compiler_params=pltpu.CompilerParams(vmem_limit_bytes=16 << 20),
        name="factor",
    )(result)


def per_device(blocks, panel, block_rows, block_cols):
    result = reduced(block_cols, block_rows.reshape(1, NB), panel.T, blocks)
    basis_t, r = factored(result)
    return basis_t.T, r


def solution(mesh):
    placed = (
        P(("grp", "dev"), None, None),
        P(("grp", "dev"), None),
        P(("grp", "dev")),
        P(("grp", "dev")),
    )
    return jax.shard_map(
        per_device,
        mesh=mesh,
        in_specs=placed,
        out_specs=(P(("grp", "dev"), None), P()),
        check_vma=False,
    )
```

```python
import functools

import jax
import jax.numpy as jnp
from jax import lax
from jax.experimental import pallas as pl
from jax.experimental.pallas import tpu as pltpu
from jax.sharding import PartitionSpec as P

MESH = pl.DeviceIdType.MESH
F32 = jnp.float32
BF16 = jnp.bfloat16
NB = 256
BS = 128
RANK = 64
ROWS = 4
NRB = 512
HALF = BS // 2
PK = HALF // 2
CHUNKS = 4
PER = NB // CHUNKS
NCOL = 16
AXES = ("x", "y", "z")
STRIDE = {"x": 1, "z": 4, "y": 32}
FLOWS = (
    (0, 0, 6, "xyz"),
    (0, 6, 11, "yzx"),
    (0, 11, 16, "zxy"),
    (1, 0, 5, "xyz"),
    (1, 5, 11, "yzx"),
    (1, 11, 16, "zxy"),
)
NF = len(FLOWS)
ORDER = (2, 3, 1, 0)
SPLITS = (((0, 2), (2, 4)), ((0, 2), (2, 4)), ((0, 1), (1, 2), (2, 3), (3, 4)))


def coords():
    g, d = lax.axis_index("grp"), lax.axis_index("dev")
    return {"x": d % 4, "z": d // 4, "y": g // 2, "c": g % 2}


def device(me, **moved):
    at = dict(me)
    at.update(moved)
    return (at["y"] * 2 + at["c"], at["z"] * 4 + at["x"])


def neighbour(me, axis, step):
    return device(me, **{axis: (me[axis] + step + 4) % 4})


def groups_of(first, end):
    out, tile = [], first
    while tile < end:
        row, within = divmod(tile, 4)
        count = min(4 - within, end - tile)
        out.append((row, within, count, tile - first))
        tile += count
    return out


def remote(src, dst, send, recv, to):
    return pltpu.make_async_remote_copy(
        src_ref=src, dst_ref=dst, send_sem=send, recv_sem=recv, device_id=to, device_id_type=MESH
    )


def reduce_kernel(*refs):
    cols_in, rows_at, panel_t, blocks, out_ref = refs[:5]
    refs = list(refs[5:])
    held, weights, sums, panel, table, meta, cols, rows_in = refs[:8]
    refs = refs[8:]
    mine_out, pair_in, a1, b1, b2, s1, a2, b12, b22, q2, c3 = (
        refs[NF * i : NF * (i + 1)] for i in range(11)
    )
    (gbuf, aux_sem, hbm_sem, pair_s, pair_r, one_s, one_r, two_s, two_r, three_s, three_r, gram_s, gram_r) = refs[NF * 11 :]
    me = coords()

    rows_copy = pltpu.make_async_copy(rows_at, rows_in, aux_sem.at[2])
    rows_copy.start()
    panel_copy = pltpu.make_async_copy(panel_t, panel, aux_sem.at[0])
    panel_copy.start()
    cols_copy = pltpu.make_async_copy(cols_in, cols, aux_sem.at[3])
    cols_copy.start()

    def load(half, c):
        part = (pl.ds(c * PER, PER), pl.ds(half * HALF, HALF))
        return pltpu.make_async_copy(blocks.at[part], held.at[part], hbm_sem.at[half, c])

    for c in range(2):
        load(0, c).start()

    barrier = pltpu.get_barrier_semaphore()
    peers = [device(me, c=1 - me["c"])]
    for axis in AXES:
        peers += [neighbour(me, axis, step) for step in (1, 2, 3)]
    for peer in peers:
        pl.semaphore_signal(barrier, inc=1, device_id=peer, device_id_type=MESH)

    rows_copy.wait()
    lane = lax.broadcasted_iota(jnp.int32, (BS, BS), 1)
    sub = lax.broadcasted_iota(jnp.int32, (BS, BS), 0)
    across = [jnp.broadcast_to(rows_in[:, i * BS : (i + 1) * BS].astype(F32), (BS, BS)) for i in range(2)]
    down = [x.T for x in across]
    for i in range(2):
        best = jnp.full((1, BS), -1, jnp.int32)
        for q in range(i + 1):
            same = across[i] == down[q]
            if q == i:
                same = same & (sub < lane)
            best = jnp.maximum(best, jnp.max(jnp.where(same, sub + q * BS, -1), axis=0, keepdims=True))
        table[:, i * BS : (i + 1) * BS] = jnp.where(best < 0, NB, best)
    for i in range(NRB // BS):
        best = jnp.full((1, BS), -1, jnp.int32)
        target = (lane + i * BS).astype(F32)
        for q in range(2):
            best = jnp.maximum(best, jnp.max(jnp.where(target == down[q], sub + q * BS, -1), axis=0, keepdims=True))
        table[:, NB + i * BS : NB + (i + 1) * BS] = jnp.where(best < 0, NB, best)
    table_copy = pltpu.make_async_copy(table, meta, aux_sem.at[1])
    table_copy.start()

    lane_low = lax.broadcasted_iota(jnp.int32, (PK, BS), 1) < RANK
    panel_copy.wait()

    for c in range(NCOL):
        p = panel[:, c * BS : (c + 1) * BS]
        high = p.astype(BF16).astype(F32)
        both = jnp.concatenate([high, p - high], axis=0).T.astype(BF16)
        weights[c, :BS, :] = both
        weights[c, BS:, :] = both
    for half in range(2):
        sums[half, NB] = jnp.zeros((PK, BS), F32)
    table_copy.wait()
    cols_copy.wait()

    def multiply(half):
        def step(c, _):
            load(half, c).wait()
            if half == 0:
                ahead = c + 2
                load(ahead // CHUNKS, ahead % CHUNKS).start()
            out = []
            for i in range(PER):
                k = c * PER + i
                x = held[k, half * HALF : (half + 1) * HALF, :]
                high = x.astype(BF16)
                low = (x - high.astype(F32)).astype(BF16)
                left = jnp.concatenate([high, low], axis=1)
                u = jnp.dot(left, weights[cols[k]], preferred_element_type=F32)
                top, bottom = u[:PK], u[PK:]
                out.append(
                    jnp.where(lane_low, top, bottom)
                    + pltpu.roll(jnp.where(lane_low, bottom, top), RANK, 1)
                )
            for i in range(PER):
                k = c * PER + i
                sums[half, k] = out[i] + sums[half, meta[0, k]]
            return 0

        lax.fori_loop(0, CHUNKS, step, 0)

    def owner(f, core, ua, ub, uc):
        half, _, _, order = FLOWS[f]
        sign = 1 if half == 0 else -1
        at = core * 16
        for axis, u in zip(order, (ua, ub, uc)):
            at = at + STRIDE[axis] * ((me[axis] + (sign * u) % 4) % 4)
        return at

    def own_rows(f, core, ua, ub, uc):
        half, first, end, _ = FLOWS[f]
        o = owner(f, core, ua, ub, uc)
        for row, within, count, offset in groups_of(first, end):
            at = meta[0, NB + o * ROWS + row]
            yield offset, count, sums[half, at, within * 8 : (within + count) * 8, :]

    def neigh(f, order_at, direction):
        half, _, _, order = FLOWS[f]
        sign = 1 if half == 0 else -1
        return neighbour(me, order[order_at], sign * direction)

    started = []

    def go(copy):
        copy.start()
        started.append(copy)
        return copy

    def pair_copy(f, ua, piece):
        at = pl.ds(piece * 2, 2)
        return remote(
            mine_out[f].at[ua, at],
            pair_in[f].at[ua, at],
            pair_s.at[f, ua, piece],
            pair_r.at[f, ua, piece],
            device(me, c=1 - me["c"]),
        )

    def fill(f, ua, piece):
        for pb in (piece * 2, piece * 2 + 1):
            for pc in range(4):
                for offset, count, value in own_rows(f, 1 - me["c"], ua, ORDER[pb], ORDER[pc]):
                    mine_out[f][ua, pb, pc, offset * 8 : (offset + count) * 8, :] = value
        go(pair_copy(f, ua, piece))

    def one_copy(f, kind, part):
        ua, buf, direction = ((2, a1, 1), (3, b1, -1), (1, b2, 1))[kind]
        lo, hi = SPLITS[kind][part]
        at = pl.ds(lo, hi - lo)
        return remote(
            pair_in[f].at[ua, at], buf[f].at[at], one_s.at[f, kind, part], one_r.at[f, kind, part], neigh(f, 0, direction)
        )

    def chip_sum(f, ua, pb, extra, out):
        for pc in range(4):
            for offset, count, value in own_rows(f, me["c"], ua, ORDER[pb], ORDER[pc]):
                rows = slice(offset * 8, (offset + count) * 8)
                value = value + pair_in[f][ua, pb, pc, rows, :]
                for e in extra:
                    value = value + e[f][pb, pc, rows, :]
                out[pc, rows, :] = value

    def begin(flows):
        for ua, piece in ((2, 0), (3, 0), (2, 1), (3, 1), (1, 0), (1, 1), (0, 0), (0, 1)):
            for f in flows:
                fill(f, ua, piece)
        for part in (0, 1):
            for kind, ua in ((0, 2), (1, 3)):
                for f in flows:
                    pair_copy(f, ua, part).wait_recv()
                    for pb in range(*SPLITS[kind][part]):
                        chip_sum(f, ua, pb, (), pair_in[f].at[ua, pb])
                    go(one_copy(f, kind, part))

    multiply(0)
    for c in range(2, CHUNKS):
        load(1, c).start()
    pl.semaphore_wait(barrier, len(peers))
    begin((0, 1, 2))
    multiply(1)
    begin((3, 4, 5))

    for part in range(4):
        for f in range(NF):
            if part % 2 == 0:
                pair_copy(f, 1, part // 2).wait_recv()
                one_copy(f, 0, part // 2).wait_recv()
            chip_sum(f, 1, part, (a1,), pair_in[f].at[1, part])
            go(one_copy(f, 2, part))

    def two_copy(f, kind):
        pb, buf, direction = ((0, a2, 1), (1, b12, -1), (2, b22, 1))[kind]
        return remote(s1[f].at[pb], buf[f], two_s.at[f, kind], two_r.at[f, kind], neigh(f, 1, direction))

    def three_copy(f, pc):
        return remote(q2[f].at[pc], c3[f].at[pc], three_s.at[f, pc], three_r.at[f, pc], neigh(f, 2, ORDER[pc]))

    for part in range(4):
        for f in range(NF):
            if part % 2 == 0:
                pair_copy(f, 0, part // 2).wait_recv()
                one_copy(f, 1, part // 2).wait_recv()
            one_copy(f, 2, part).wait_recv()
            chip_sum(f, 0, part, (b1, b2), s1[f].at[part])
            if part < 2:
                go(two_copy(f, part))
            elif part == 2:
                two_copy(f, 0).wait_recv()
                s1[f][2] = s1[f][2] + a2[f][...]
                go(two_copy(f, 2))
    for f in range(NF):
        two_copy(f, 1).wait_recv()
        two_copy(f, 2).wait_recv()
        q2[f][...] = s1[f][3] + b12[f][...] + b22[f][...]
        for pc in range(3):
            go(three_copy(f, pc))
    for f in range(NF):
        half, first, end, _ = FLOWS[f]
        for pc in range(3):
            three_copy(f, pc).wait_recv()
        out_ref[half * 128 + first * 8 : half * 128 + end * 8, :] = (
            q2[f][3] + c3[f][0] + (c3[f][1] + c3[f][2])
        )

    prod = out_ref[:256, :]
    both = lax.dot_general(
        prod, prod, (((0,), (0,)), ((), ())), precision=lax.Precision.HIGHEST, preferred_element_type=F32
    )
    upper, lower = both[:RANK], both[RANK:]
    in_low = upper + pltpu.roll(lower, RANK, 1)
    in_high = pltpu.roll(upper, RANK, 1) + lower
    gbuf[0, 0] = jnp.where(lane_low, in_low[:PK], in_high[PK:]) * (1.0 / (NRB * BS))

    copy = go(remote(gbuf.at[0, 0], gbuf.at[0, 1], gram_s.at[0, 0], gram_r.at[0, 0], device(me, c=1 - me["c"])))
    copy.wait_recv()
    total = gbuf[0, 0] + gbuf[0, 1]
    for i, axis in enumerate(AXES):
        gbuf[i + 1, 0] = total
        copies = [
            go(
                remote(
                    gbuf.at[i + 1, 0],
                    gbuf.at[i + 1, step],
                    gram_s.at[i + 1, step - 1],
                    gram_r.at[i + 1, step - 1],
                    neighbour(me, axis, step),
                )
            )
            for step in (1, 2, 3)
        ]
        for copy in copies:
            copy.wait_recv()
        total = (gbuf[i + 1, 0] + gbuf[i + 1, 2]) + (gbuf[i + 1, 1] + gbuf[i + 1, 3])
    out_ref[256:, :] = total
    for copy in started:
        copy.wait_send()


def factor_kernel(in_ref, basis_ref, r_ref):
    lane = lax.broadcasted_iota(jnp.int32, (8, BS), 1)
    sub = lax.broadcasted_iota(jnp.int32, (8, BS), 0)
    packed = in_ref[256:, :]
    turned = pltpu.roll(packed, RANK, 1)
    tiles = []
    for t in range(8):
        half = packed if t < 4 else turned
        g = half[(t % 4) * 8 : (t % 4 + 1) * 8, :]
        eye = (lane - RANK == sub + t * 8).astype(F32)
        tiles.append(jnp.where(lane < RANK, g, eye))

    def row_of(x, j):
        return jnp.broadcast_to(x[j : j + 1, :], (8, BS))

    def column_of(x, j):
        return jnp.broadcast_to(x[:, j : j + 1], (8, BS))

    done = []
    for t in range(8):
        cols = [column_of(tiles[t], 8 * t + j) for j in range(8)]
        rest = {u: [column_of(tiles[u], 8 * t + j) for j in range(8)] for u in range(t + 1, 8)}
        forward = full = tiles[t]
        pivots = inverses = jnp.ones((8, BS), F32)
        for j in range(8):
            pivot = row_of(cols[j], j)
            inverse = 1.0 / pivot
            pivots = jnp.where(sub == j, pivot, pivots)
            inverses = jnp.where(sub == j, inverse, inverses)
            c = cols[j] * inverse
            others = jnp.where(sub == j, 0.0, c)
            for k in range(j + 1, 8):
                cols[k] = cols[k] - others * row_of(cols[k], j)
            row = row_of(full, j)
            forward = forward - jnp.where(sub > j, c, 0.0) * row
            full = full - others * row
        full = full * inverses
        rows = [row_of(full, j) for j in range(8)]
        for u in range(t + 1, 8):
            p = [rest[u][j] * rows[j] for j in range(8)]
            p = [p[0] + p[1], p[2] + p[3], p[4] + p[5], p[6] + p[7]]
            tiles[u] = tiles[u] - ((p[0] + p[1]) + (p[2] + p[3]))
        scale = lax.rsqrt(pivots)
        done.append(forward * (scale * (1.5 - 0.5 * pivots * scale * scale)))
    scaled = jnp.concatenate(done, axis=0)
    lane = lax.broadcasted_iota(jnp.int32, (RANK, BS), 1)
    sub = lax.broadcasted_iota(jnp.int32, (RANK, BS), 0)
    r_ref[...] = jnp.where(lane >= sub, scaled, 0.0)[:, :RANK]
    inverse = pltpu.roll(jnp.where(lane >= RANK, scaled, 0.0), RANK, 1)
    prod = in_ref[:256, :]
    turned = pltpu.roll(prod, RANK, 1)
    for r in range(ROWS):
        part = jnp.concatenate(
            [x[half * BS + r * PK : half * BS + (r + 1) * PK] for half in range(2) for x in (prod, turned)], axis=0
        )
        basis_ref[:, r * BS : (r + 1) * BS] = lax.dot_general(
            inverse, part, (((1,), (1,)), ((), ())), precision=lax.Precision.HIGHEST, preferred_element_type=F32
        )


def reduced(cols, rows_in, panel_t, blocks):
    rows = [(end - first) * 8 for _, first, end, _ in FLOWS]

    def per_flow(*lead):
        return [pltpu.VMEM((*lead, n, BS), F32) for n in rows]

    dma = pltpu.SemaphoreType.DMA
    scratch = [
        pltpu.VMEM((NB, BS, BS), F32),
        pltpu.VMEM((16, 2 * BS, BS), BF16),
        pltpu.VMEM((2, NB + 1, PK, BS), F32),
        pltpu.VMEM((RANK, NCOL * BS), F32),
        pltpu.VMEM((1, NB + NRB), jnp.int32),
        pltpu.SMEM((1, NB + NRB), jnp.int32),
        pltpu.SMEM((NB,), jnp.int32),
        pltpu.VMEM((1, NB), jnp.int32),
        *per_flow(4, 4, 4),
        *per_flow(4, 4, 4),
        *per_flow(4, 4),
        *per_flow(4, 4),
        *per_flow(4, 4),
        *per_flow(4, 4),
        *per_flow(4),
        *per_flow(4),
        *per_flow(4),
        *per_flow(4),
        *per_flow(3),
        pltpu.VMEM((4, 4, PK, BS), F32),
        dma((4,)),
        dma((2, CHUNKS)),
        dma((NF, 4, 2)),
        dma((NF, 4, 2)),
        dma((NF, 3, 4)),
        dma((NF, 3, 4)),
        dma((NF, 3)),
        dma((NF, 3)),
        dma((NF, 3)),
        dma((NF, 3)),
        dma((4, 3)),
        dma((4, 3)),
    ]
    return pl.pallas_call(
        reduce_kernel,
        out_shape=jax.ShapeDtypeStruct((256 + PK, BS), F32),
        in_specs=[
            pl.BlockSpec(memory_space=pl.ANY),
            pl.BlockSpec(memory_space=pl.ANY),
            pl.BlockSpec(memory_space=pl.ANY),
            pl.BlockSpec(memory_space=pl.ANY),
        ],
        out_specs=pl.BlockSpec(memory_space=pltpu.VMEM),
        scratch_shapes=scratch,
        compiler_params=pltpu.CompilerParams(collective_id=0, has_side_effects=True, vmem_limit_bytes=60 << 20),
        name="reduce",
    )(cols, rows_in, panel_t, blocks)


def factored(result):
    vmem = pl.BlockSpec(memory_space=pltpu.VMEM)
    return pl.pallas_call(
        factor_kernel,
        out_shape=(jax.ShapeDtypeStruct((RANK, 512), F32), jax.ShapeDtypeStruct((RANK, RANK), F32)),
        in_specs=[vmem],
        out_specs=(vmem, vmem),
        compiler_params=pltpu.CompilerParams(vmem_limit_bytes=16 << 20),
        name="factor",
    )(result)


def per_device(blocks, panel, block_rows, block_cols):
    result = reduced(block_cols, block_rows.reshape(1, NB), panel.T, blocks)
    basis_t, r = factored(result)
    return basis_t.T, r


def solution(mesh):
    placed = (
        P(("grp", "dev"), None, None),
        P(("grp", "dev"), None),
        P(("grp", "dev")),
        P(("grp", "dev")),
    )
    return jax.shard_map(
        per_device,
        mesh=mesh,
        in_specs=placed,
        out_specs=(P(("grp", "dev"), None), P()),
        check_vma=False,
    )
```

```python
import functools

import jax
import jax.numpy as jnp
from jax import lax
from jax.experimental import pallas as pl
from jax.experimental.pallas import tpu as pltpu
from jax.sharding import PartitionSpec as P

MESH = pl.DeviceIdType.MESH
F32 = jnp.float32
BF16 = jnp.bfloat16
NB = 256
BS = 128
RANK = 64
ROWS = 4
NRB = 512
HALF = BS // 2
PK = HALF // 2
CHUNKS = 4
PER = NB // CHUNKS
NCOL = 16
AXES = ("x", "y", "z")
STRIDE = {"x": 1, "z": 4, "y": 32}
FLOWS = (
    (0, 0, 6, "xyz"),
    (0, 6, 11, "yzx"),
    (0, 11, 16, "zxy"),
    (1, 0, 5, "xyz"),
    (1, 5, 11, "yzx"),
    (1, 11, 16, "zxy"),
)
NF = len(FLOWS)
ORDER = (2, 3, 1, 0)
SPLITS = (((0, 2), (2, 4)), ((0, 2), (2, 4)), ((0, 1), (1, 2), (2, 3), (3, 4)))


def coords():
    g, d = lax.axis_index("grp"), lax.axis_index("dev")
    return {"x": d % 4, "z": d // 4, "y": g // 2, "c": g % 2}


def device(me, **moved):
    at = dict(me)
    at.update(moved)
    return (at["y"] * 2 + at["c"], at["z"] * 4 + at["x"])


def neighbour(me, axis, step):
    return device(me, **{axis: (me[axis] + step + 4) % 4})


def groups_of(first, end):
    out, tile = [], first
    while tile < end:
        row, within = divmod(tile, 4)
        count = min(4 - within, end - tile)
        out.append((row, within, count, tile - first))
        tile += count
    return out


def remote(src, dst, send, recv, to):
    return pltpu.make_async_remote_copy(
        src_ref=src, dst_ref=dst, send_sem=send, recv_sem=recv, device_id=to, device_id_type=MESH
    )


def reduce_kernel(*refs):
    cols_in, rows_at, panel_t, blocks, out_ref = refs[:5]
    refs = list(refs[5:])
    held, weights, sums, panel, table, meta, cols, rows_in = refs[:8]
    refs = refs[8:]
    mine_out, pair_in, a1, b1, b2, s1, a2, b12, b22, q2, c3 = (
        refs[NF * i : NF * (i + 1)] for i in range(11)
    )
    (gbuf, aux_sem, hbm_sem, pair_s, pair_r, one_s, one_r, two_s, two_r, three_s, three_r, gram_s, gram_r) = refs[NF * 11 :]
    me = coords()

    rows_copy = pltpu.make_async_copy(rows_at, rows_in, aux_sem.at[2])
    rows_copy.start()
    panel_copy = pltpu.make_async_copy(panel_t, panel, aux_sem.at[0])
    panel_copy.start()
    cols_copy = pltpu.make_async_copy(cols_in, cols, aux_sem.at[3])
    cols_copy.start()

    def load(half, c):
        part = (pl.ds(c * PER, PER), pl.ds(half * HALF, HALF))
        return pltpu.make_async_copy(blocks.at[part], held.at[part], hbm_sem.at[half, c])

    for c in range(2):
        load(0, c).start()

    barrier = pltpu.get_barrier_semaphore()
    peers = [device(me, c=1 - me["c"])]
    for axis in AXES:
        peers += [neighbour(me, axis, step) for step in (1, 2, 3)]
    for peer in peers:
        pl.semaphore_signal(barrier, inc=1, device_id=peer, device_id_type=MESH)

    rows_copy.wait()
    lane = lax.broadcasted_iota(jnp.int32, (BS, BS), 1)
    sub = lax.broadcasted_iota(jnp.int32, (BS, BS), 0)
    across = [jnp.broadcast_to(rows_in[:, i * BS : (i + 1) * BS].astype(F32), (BS, BS)) for i in range(2)]
    down = [x.T for x in across]
    for i in range(2):
        best = jnp.full((1, BS), -1, jnp.int32)
        for q in range(i + 1):
            same = across[i] == down[q]
            if q == i:
                same = same & (sub < lane)
            best = jnp.maximum(best, jnp.max(jnp.where(same, sub + q * BS, -1), axis=0, keepdims=True))
        table[:, i * BS : (i + 1) * BS] = jnp.where(best < 0, NB, best)
    for i in range(NRB // BS):
        best = jnp.full((1, BS), -1, jnp.int32)
        target = (lane + i * BS).astype(F32)
        for q in range(2):
            best = jnp.maximum(best, jnp.max(jnp.where(target == down[q], sub + q * BS, -1), axis=0, keepdims=True))
        table[:, NB + i * BS : NB + (i + 1) * BS] = jnp.where(best < 0, NB, best)
    table_copy = pltpu.make_async_copy(table, meta, aux_sem.at[1])
    table_copy.start()

    lane_low = lax.broadcasted_iota(jnp.int32, (PK, BS), 1) < RANK
    panel_copy.wait()

    for c in range(NCOL):
        p = panel[:, c * BS : (c + 1) * BS]
        high = p.astype(BF16).astype(F32)
        both = jnp.concatenate([high, p - high], axis=0).T.astype(BF16)
        weights[c, :BS, :] = both
        weights[c, BS:, :] = both
    for half in range(2):
        sums[half, NB] = jnp.zeros((PK, BS), F32)
    table_copy.wait()
    cols_copy.wait()

    def multiply(half):
        def step(c, _):
            load(half, c).wait()
            if half == 0:
                ahead = c + 2
                load(ahead // CHUNKS, ahead % CHUNKS).start()
            out = []
            for i in range(PER):
                k = c * PER + i
                x = held[k, half * HALF : (half + 1) * HALF, :]
                high = x.astype(BF16)
                low = (x - high.astype(F32)).astype(BF16)
                left = jnp.concatenate([high, low], axis=1)
                u = jnp.dot(left, weights[cols[k]], preferred_element_type=F32)
                top, bottom = u[:PK], u[PK:]
                out.append(
                    jnp.where(lane_low, top, bottom)
                    + pltpu.roll(jnp.where(lane_low, bottom, top), RANK, 1)
                )
            for i in range(PER):
                k = c * PER + i
                sums[half, k] = out[i] + sums[half, meta[0, k]]
            return 0

        lax.fori_loop(0, CHUNKS, step, 0)

    def owner(f, core, ua, ub, uc):
        half, _, _, order = FLOWS[f]
        sign = 1 if half == 0 else -1
        at = core * 16
        for axis, u in zip(order, (ua, ub, uc)):
            at = at + STRIDE[axis] * ((me[axis] + (sign * u) % 4) % 4)
        return at

    def own_rows(f, core, ua, ub, uc):
        half, first, end, _ = FLOWS[f]
        o = owner(f, core, ua, ub, uc)
        for row, within, count, offset in groups_of(first, end):
            at = meta[0, NB + o * ROWS + row]
            yield offset, count, sums[half, at, within * 8 : (within + count) * 8, :]

    def neigh(f, order_at, direction):
        half, _, _, order = FLOWS[f]
        sign = 1 if half == 0 else -1
        return neighbour(me, order[order_at], sign * direction)

    started = []

    def go(copy):
        copy.start()
        started.append(copy)
        return copy

    def pair_copy(f, ua, piece):
        at = pl.ds(piece * 2, 2)
        return remote(
            mine_out[f].at[ua, at],
            pair_in[f].at[ua, at],
            pair_s.at[f, ua, piece],
            pair_r.at[f, ua, piece],
            device(me, c=1 - me["c"]),
        )

    def fill(f, ua, piece):
        for pb in (piece * 2, piece * 2 + 1):
            for pc in range(4):
                for offset, count, value in own_rows(f, 1 - me["c"], ua, ORDER[pb], ORDER[pc]):
                    mine_out[f][ua, pb, pc, offset * 8 : (offset + count) * 8, :] = value
        go(pair_copy(f, ua, piece))

    def one_copy(f, kind, part):
        ua, buf, direction = ((2, a1, 1), (3, b1, -1), (1, b2, 1))[kind]
        lo, hi = SPLITS[kind][part]
        at = pl.ds(lo, hi - lo)
        return remote(
            pair_in[f].at[ua, at], buf[f].at[at], one_s.at[f, kind, part], one_r.at[f, kind, part], neigh(f, 0, direction)
        )

    def chip_sum(f, ua, pb, extra, out):
        for pc in range(4):
            for offset, count, value in own_rows(f, me["c"], ua, ORDER[pb], ORDER[pc]):
                rows = slice(offset * 8, (offset + count) * 8)
                value = value + pair_in[f][ua, pb, pc, rows, :]
                for e in extra:
                    value = value + e[f][pb, pc, rows, :]
                out[pc, rows, :] = value

    def begin(flows):
        for ua, piece in ((2, 0), (3, 0), (2, 1), (3, 1), (1, 0), (1, 1), (0, 0), (0, 1)):
            for f in flows:
                fill(f, ua, piece)
        for part in (0, 1):
            for kind, ua in ((0, 2), (1, 3)):
                for f in flows:
                    pair_copy(f, ua, part).wait_recv()
                    for pb in range(*SPLITS[kind][part]):
                        chip_sum(f, ua, pb, (), pair_in[f].at[ua, pb])
                    go(one_copy(f, kind, part))

    multiply(0)
    for c in range(2, CHUNKS):
        load(1, c).start()
    pl.semaphore_wait(barrier, len(peers))
    begin((0, 1, 2))
    multiply(1)
    begin((3, 4, 5))

    for part in range(4):
        for f in range(NF):
            if part % 2 == 0:
                pair_copy(f, 1, part // 2).wait_recv()
                one_copy(f, 0, part // 2).wait_recv()
            chip_sum(f, 1, part, (a1,), pair_in[f].at[1, part])
            go(one_copy(f, 2, part))

    def two_copy(f, kind):
        pb, buf, direction = ((0, a2, 1), (1, b12, -1), (2, b22, 1))[kind]
        return remote(s1[f].at[pb], buf[f], two_s.at[f, kind], two_r.at[f, kind], neigh(f, 1, direction))

    def three_copy(f, pc):
        return remote(q2[f].at[pc], c3[f].at[pc], three_s.at[f, pc], three_r.at[f, pc], neigh(f, 2, ORDER[pc]))

    for part in range(4):
        for f in range(NF):
            if part % 2 == 0:
                pair_copy(f, 0, part // 2).wait_recv()
                one_copy(f, 1, part // 2).wait_recv()
            one_copy(f, 2, part).wait_recv()
            chip_sum(f, 0, part, (b1, b2), s1[f].at[part])
            if part < 2:
                go(two_copy(f, part))
            elif part == 2:
                two_copy(f, 0).wait_recv()
                s1[f][2] = s1[f][2] + a2[f][...]
                go(two_copy(f, 2))
    for f in range(NF):
        two_copy(f, 1).wait_recv()
        two_copy(f, 2).wait_recv()
        q2[f][...] = s1[f][3] + b12[f][...] + b22[f][...]
        for pc in range(3):
            go(three_copy(f, pc))
    for f in range(NF):
        half, first, end, _ = FLOWS[f]
        for pc in range(3):
            three_copy(f, pc).wait_recv()
        out_ref[half * 128 + first * 8 : half * 128 + end * 8, :] = (
            q2[f][3] + c3[f][0] + (c3[f][1] + c3[f][2])
        )

    prod = out_ref[:256, :]
    both = lax.dot_general(
        prod, prod, (((0,), (0,)), ((), ())), precision=lax.Precision.HIGHEST, preferred_element_type=F32
    )
    upper, lower = both[:RANK], both[RANK:]
    in_low = upper + pltpu.roll(lower, RANK, 1)
    in_high = pltpu.roll(upper, RANK, 1) + lower
    gbuf[0, 0] = jnp.where(lane_low, in_low[:PK], in_high[PK:]) * (1.0 / (NRB * BS))

    copy = go(remote(gbuf.at[0, 0], gbuf.at[0, 1], gram_s.at[0, 0], gram_r.at[0, 0], device(me, c=1 - me["c"])))
    copy.wait_recv()
    total = gbuf[0, 0] + gbuf[0, 1]
    for i, axis in enumerate(AXES):
        gbuf[i + 1, 0] = total
        copies = [
            go(
                remote(
                    gbuf.at[i + 1, 0],
                    gbuf.at[i + 1, step],
                    gram_s.at[i + 1, step - 1],
                    gram_r.at[i + 1, step - 1],
                    neighbour(me, axis, step),
                )
            )
            for step in (1, 2, 3)
        ]
        for copy in copies:
            copy.wait_recv()
        total = (gbuf[i + 1, 0] + gbuf[i + 1, 2]) + (gbuf[i + 1, 1] + gbuf[i + 1, 3])
    out_ref[256:, :] = total
    for copy in started:
        copy.wait_send()


def factor_kernel(in_ref, basis_ref, r_ref, gram, prod_in, sem):
    lane = lax.broadcasted_iota(jnp.int32, (8, BS), 1)
    sub = lax.broadcasted_iota(jnp.int32, (8, BS), 0)
    gram_copy = pltpu.make_async_copy(in_ref.at[pl.ds(256, PK)], gram, sem.at[0])
    gram_copy.start()
    prod_copy = pltpu.make_async_copy(in_ref.at[pl.ds(0, 256)], prod_in, sem.at[1])
    prod_copy.start()
    gram_copy.wait()
    packed = gram[...]
    turned = pltpu.roll(packed, RANK, 1)
    tiles = []
    for t in range(8):
        half = packed if t < 4 else turned
        g = half[(t % 4) * 8 : (t % 4 + 1) * 8, :]
        eye = (lane - RANK == sub + t * 8).astype(F32)
        tiles.append(jnp.where(lane < RANK, g, eye))

    def row_of(x, j):
        return jnp.broadcast_to(x[j : j + 1, :], (8, BS))

    def column_of(x, j):
        return jnp.broadcast_to(x[:, j : j + 1], (8, BS))

    done = []
    for t in range(8):
        cols = [column_of(tiles[t], 8 * t + j) for j in range(8)]
        rest = {u: [column_of(tiles[u], 8 * t + j) for j in range(8)] for u in range(t + 1, 8)}
        forward = full = tiles[t]
        pivots = inverses = jnp.ones((8, BS), F32)
        for j in range(8):
            pivot = row_of(cols[j], j)
            inverse = 1.0 / pivot
            pivots = jnp.where(sub == j, pivot, pivots)
            inverses = jnp.where(sub == j, inverse, inverses)
            c = cols[j] * inverse
            others = jnp.where(sub == j, 0.0, c)
            for k in range(j + 1, 8):
                cols[k] = cols[k] - others * row_of(cols[k], j)
            row = row_of(full, j)
            forward = forward - jnp.where(sub > j, c, 0.0) * row
            full = full - others * row
        full = full * inverses
        rows = [row_of(full, j) for j in range(8)]
        for u in range(t + 1, 8):
            p = [rest[u][j] * rows[j] for j in range(8)]
            p = [p[0] + p[1], p[2] + p[3], p[4] + p[5], p[6] + p[7]]
            tiles[u] = tiles[u] - ((p[0] + p[1]) + (p[2] + p[3]))
        scale = lax.rsqrt(pivots)
        done.append(forward * (scale * (1.5 - 0.5 * pivots * scale * scale)))
    scaled = jnp.concatenate(done, axis=0)
    lane = lax.broadcasted_iota(jnp.int32, (RANK, BS), 1)
    sub = lax.broadcasted_iota(jnp.int32, (RANK, BS), 0)
    r_ref[...] = jnp.where(lane >= sub, scaled, 0.0)[:, :RANK]
    inverse = pltpu.roll(jnp.where(lane >= RANK, scaled, 0.0), RANK, 1)
    prod_copy.wait()
    prod = prod_in[...]
    turned = pltpu.roll(prod, RANK, 1)
    for r in range(ROWS):
        part = jnp.concatenate(
            [x[half * BS + r * PK : half * BS + (r + 1) * PK] for half in range(2) for x in (prod, turned)], axis=0
        )
        basis_ref[:, r * BS : (r + 1) * BS] = lax.dot_general(
            inverse, part, (((1,), (1,)), ((), ())), precision=lax.Precision.HIGHEST, preferred_element_type=F32
        )


def reduced(cols, rows_in, panel_t, blocks):
    rows = [(end - first) * 8 for _, first, end, _ in FLOWS]

    def per_flow(*lead):
        return [pltpu.VMEM((*lead, n, BS), F32) for n in rows]

    dma = pltpu.SemaphoreType.DMA
    scratch = [
        pltpu.VMEM((NB, BS, BS), F32),
        pltpu.VMEM((16, 2 * BS, BS), BF16),
        pltpu.VMEM((2, NB + 1, PK, BS), F32),
        pltpu.VMEM((RANK, NCOL * BS), F32),
        pltpu.VMEM((1, NB + NRB), jnp.int32),
        pltpu.SMEM((1, NB + NRB), jnp.int32),
        pltpu.SMEM((NB,), jnp.int32),
        pltpu.VMEM((1, NB), jnp.int32),
        *per_flow(4, 4, 4),
        *per_flow(4, 4, 4),
        *per_flow(4, 4),
        *per_flow(4, 4),
        *per_flow(4, 4),
        *per_flow(4, 4),
        *per_flow(4),
        *per_flow(4),
        *per_flow(4),
        *per_flow(4),
        *per_flow(3),
        pltpu.VMEM((4, 4, PK, BS), F32),
        dma((4,)),
        dma((2, CHUNKS)),
        dma((NF, 4, 2)),
        dma((NF, 4, 2)),
        dma((NF, 3, 4)),
        dma((NF, 3, 4)),
        dma((NF, 3)),
        dma((NF, 3)),
        dma((NF, 3)),
        dma((NF, 3)),
        dma((4, 3)),
        dma((4, 3)),
    ]
    return pl.pallas_call(
        reduce_kernel,
        out_shape=jax.ShapeDtypeStruct((256 + PK, BS), F32),
        in_specs=[
            pl.BlockSpec(memory_space=pl.ANY),
            pl.BlockSpec(memory_space=pl.ANY),
            pl.BlockSpec(memory_space=pl.ANY),
            pl.BlockSpec(memory_space=pl.ANY),
        ],
        out_specs=pl.BlockSpec(memory_space=pltpu.VMEM),
        scratch_shapes=scratch,
        compiler_params=pltpu.CompilerParams(collective_id=0, has_side_effects=True, vmem_limit_bytes=60 << 20),
        name="reduce",
    )(cols, rows_in, panel_t, blocks)


def factored(result):
    vmem = pl.BlockSpec(memory_space=pltpu.VMEM)
    return pl.pallas_call(
        factor_kernel,
        out_shape=(jax.ShapeDtypeStruct((RANK, 512), F32), jax.ShapeDtypeStruct((RANK, RANK), F32)),
        in_specs=[pl.BlockSpec(memory_space=pl.ANY)],
        out_specs=(vmem, vmem),
        scratch_shapes=[pltpu.VMEM((PK, BS), F32), pltpu.VMEM((256, BS), F32), pltpu.SemaphoreType.DMA((2,))],
        compiler_params=pltpu.CompilerParams(vmem_limit_bytes=60 << 20),
        name="factor",
    )(result)


def per_device(blocks, panel, block_rows, block_cols):
    result = reduced(block_cols, block_rows.reshape(1, NB), panel.T, blocks)
    basis_t, r = factored(result)
    return basis_t.T, r


def solution(mesh):
    placed = (
        P(("grp", "dev"), None, None),
        P(("grp", "dev"), None),
        P(("grp", "dev")),
        P(("grp", "dev")),
    )
    return jax.shard_map(
        per_device,
        mesh=mesh,
        in_specs=placed,
        out_specs=(P(("grp", "dev"), None), P()),
        check_vma=False,
    )
```
